32 devices in a mesh: dp: 2 (over core), cent: 16 (over z, y, x).
Axes of the slice: x: 2, y: 2, z: 4, core: 2. Of those that a mesh axis runs over, the one named last changes fastest.
Arguments:
- points: bfloat16 [4096, 768], P(('dp', 'cent')), may hold values from -16 to 16
- centroids: float32 [32768, 768], P(('dp', 'cent')), may hold values from -1.5 to 1.5
Outputs:
- new_centroids: float32 [32768, 768], P(('dp', 'cent'))
- log_total: float32 [4096], P(('dp', 'cent'))
The draws below stay inside these ranges and needn't reach their ends.
All inputs are finite; a program needn't handle non-finite values.
Results may differ from the reference program's by a relative error of at most 0.0088.
Values may be sent and summed in bfloat16 or wider, within the bound.
A program may use at most 128 MiB of HBM per device.

```python
import math
import jax
import jax.numpy as jnp
from jax import lax

D = 768
K = 32768
NPTS = 4096


pair_count = 6


def centroid_table(key):
    first_key = jax.random.fold_in(key, 11)
    table = jax.random.normal(first_key, (K, D), jnp.float32) * 0.25
    return jnp.clip(table, -1.5, 1.5)


def draw_centroids(key, part):
    return centroid_table(key)


def aligned_rows(key, values):
    table = centroid_table(key)
    chosen = jax.random.randint(jax.random.fold_in(key, 12), (pair_count,), 0, K - 1)
    targets = jax.random.randint(jax.random.fold_in(key, 24), (pair_count,), 0, NPTS)
    rows = table[chosen]
    row_norm = jnp.sum(rows * rows, axis=1)
    wanted = jnp.array([120.0, 160.0, 220.0, 120.0, 160.0, 220.0], jnp.float32)
    strength = (wanted * math.sqrt(D) / (7.0 * row_norm) + 1.0) * 0.5
    return values.at[targets].set(rows * strength[:, None])


def draw_points(key, part):
    row_scale = jnp.exp(jax.random.uniform(jax.random.fold_in(key, 21), (NPTS, 1), jnp.float32, -1.0498221, 1.252763))
    values = jax.random.normal(jax.random.fold_in(key, 22), (NPTS, D), jnp.float32) * row_scale
    values = aligned_rows(key, values)
    return jnp.clip(values, -16.0, 16.0).astype(jnp.bfloat16)


def setup_inputs(seed: int = 0) -> dict:
    splits = jax.random.split(jax.random.key(seed), 3)
    points = draw_points(jax.random.fold_in(splits[2], 71), 0)
    centroids = draw_centroids(jax.random.fold_in(splits[2], 71), 0)
    return dict(points=points, centroids=centroids)


def fold_stats(running, scores):
    old_max, old_sum = running
    new_max = jnp.maximum(old_max, lax.optimization_barrier(jnp.max(scores, axis=1)))
    new_sum = old_sum * jnp.exp(old_max - new_max) + lax.optimization_barrier(jnp.sum(jnp.exp(scores - new_max[:, None]), axis=1))
    return (new_max, new_sum)

def reference(points, centroids):
    copies = centroids.astype(jnp.bfloat16)
    copies = lax.optimization_barrier(copies).astype(jnp.float32)
    sq_norm = lax.optimization_barrier(jnp.sum(copies * copies, axis=1))
    features = points.astype(jnp.float32)
    score_scale = 7.0 / math.sqrt(D)
    block_count = K // 512
    stacked = copies.reshape(block_count, 512, D)
    norm_rows = sq_norm.reshape(block_count, 512)

    def scores_of(table, norms):
        products = jnp.dot(features, table.T, precision=lax.Precision.HIGHEST)
        return (2.0 * products - norms[None, :]) * score_scale

    def scan_step(running, item):
        table, norms = item
        return (fold_stats(running, scores_of(table, norms)), None)
    start = (jnp.full((NPTS,), -1e+30, jnp.float32), jnp.zeros((NPTS,), jnp.float32))
    (run_max, run_sum), unused = lax.scan(scan_step, start, (stacked, norm_rows))
    log_total = run_max + jnp.log(run_sum)

    def block_sums(item):
        table, norms = item
        weights = jnp.exp(scores_of(table, norms) - log_total[:, None]).astype(jnp.bfloat16)
        weights = lax.optimization_barrier(weights).astype(jnp.float32)
        return (jnp.dot(weights.T, features, precision=lax.Precision.HIGHEST), lax.optimization_barrier(jnp.sum(weights, axis=0)))
    sums, counts = lax.map(block_sums, (stacked, norm_rows))
    sums = sums.reshape(K, D)
    counts = counts.reshape(K)
    new_centroids = (sums + centroids) / (counts[:, None] + 1.0)
    return (new_centroids, log_total)
```

```python
import functools
import math

import jax
import jax.numpy as jnp
from jax import lax
from jax.experimental import pallas as pl
from jax.experimental.pallas import tpu as pltpu
from jax.sharding import PartitionSpec as P

MESH = pl.DeviceIdType.MESH
LOG2E = 1.4426950408889634
LN2 = 0.6931471805599453
Z_AXIS, Y_AXIS, X_AXIS = 0, 1, 2
SHARES = (
    (0.5, (Z_AXIS, X_AXIS, Y_AXIS)),
    (0.5, (Z_AXIS, Y_AXIS, X_AXIS)),
)
SEND_DEPTH = 16
NEAREST = (
    (0, 0, 0), (0, 0, 1), (0, 1, 0), (1, 0, 0), (0, 1, 1), (1, 0, 1), (1, 1, 0), (2, 0, 0),
    (1, 1, 1), (2, 0, 1), (2, 1, 0), (3, 0, 0), (2, 1, 1), (3, 0, 1), (3, 1, 0), (3, 1, 1),
)


def chip_grid(chips):
    sizes = [1, 1, 1]
    axis = 0
    order = (Z_AXIS, Y_AXIS, X_AXIS)
    left = chips
    if chips >= 16:
        sizes[0] = 4
        left //= 4
    while left > 1:
        sizes[order[axis % 3]] *= 2 if (chips < 16 or axis % 3) else 1
        left = chips // (sizes[0] * sizes[1] * sizes[2])
        axis += 1
    return tuple(sizes)


def row_parts(rows):
    parts, first = [], 0
    for index, (share, order) in enumerate(SHARES):
        last = rows if index == len(SHARES) - 1 else first + int(share * rows) // 16 * 16
        parts.append((first, last - first, order))
        first = last
    return parts


def ranked(rank, at, size):
    if size == 1:
        return at * 0
    if size == 2:
        return lax.rem(at + rank, 2)
    low = jnp.where(at < 2, at, 3 - at)
    place = jnp.where(low == 0, rank, jnp.where(rank == 3, 3, lax.rem(rank + 1, 3)))
    return jnp.where(at < 2, place, 3 - place)


def source_of(step, at, grid):
    nz, ny, nx = grid
    if grid == (4, 2, 2):
        ranks = []
        for axis in range(3):
            value = jnp.int32(NEAREST[0][axis])
            for index in range(1, len(NEAREST)):
                value = jnp.where(step == index, NEAREST[index][axis], value)
            ranks.append(value)
    else:
        ranks = [step // (ny * nx), (step // nx) % ny, step % nx]
    return [ranked(rank, place, size) for rank, place, size in zip(ranks, at, grid)]


def kernel(
    grid, parts, alpha, chunk,
    points_ref, cent_hbm, out_hbm, total_ref,
    xbuf, acc, copies, norms, ebuf, weights, counts, local_max,
    stat_out, stat_in, totals,
    load_sem, store_sem, send_sem, recv_sem, side_send, side_recv,
    stat_send, stat_recv, total_send, total_recv,
):
    nz, ny, nx = grid
    chips = nz * ny * nx
    devices = 2 * chips
    core = lax.axis_index("dp")
    chip = lax.axis_index("cent")
    me = chip * 2 + core
    at = [chip // (ny * nx), (chip // nx) % ny, chip % nx]
    strides = (ny * nx, nx, 1)
    own_rows = copies.shape[0]

    load = pltpu.make_async_copy(cent_hbm, acc, load_sem)
    load.start()

    barrier = pltpu.get_barrier_semaphore()

    def greet(index, carry):
        other = lax.rem(me + index, devices)
        pl.semaphore_signal(
            barrier, inc=1, device_id=(lax.rem(other, 2), other // 2), device_id_type=MESH
        )
        return carry

    lax.fori_loop(1, devices, greet, 0)
    xbuf[chip, core] = points_ref[...]
    pl.semaphore_wait(barrier, devices - 1)

    def part_copy(source, slot, link, part, target):
        first, rows, _ = parts[part]
        piece = xbuf.at[source, core, pl.ds(first, rows)]
        return pltpu.make_async_remote_copy(
            src_ref=piece,
            dst_ref=piece,
            send_sem=send_sem.at[slot, link],
            recv_sem=recv_sem.at[source, part],
            device_id=(core, target),
            device_id_type=MESH,
        )

    def side_copy(source):
        return pltpu.make_async_remote_copy(
            src_ref=xbuf.at[source, core],
            dst_ref=xbuf.at[source, core],
            send_sem=side_send.at[source],
            recv_sem=side_recv.at[source],
            device_id=(1 - core, chip),
            device_id_type=MESH,
        )

    def index_of(place):
        return place[0] * strides[0] + place[1] * strides[1] + place[2]

    def forwards(step, act):
        place = source_of(step, at, grid)
        source = index_of(place)
        slot = lax.rem(step, SEND_DEPTH)
        link = 0
        for part, (_, _, order) in enumerate(parts):
            for position, axis in enumerate(order):
                if grid[axis] == 1:
                    continue
                clear = None
                for later in order[position + 1 :]:
                    if grid[later] > 1:
                        same = place[later] == at[later]
                        clear = same if clear is None else jnp.logical_and(clear, same)
                if grid[axis] == 2:
                    options = [(place[axis] == at[axis], (1 - 2 * at[axis]) * strides[axis])]
                else:
                    options = [
                        (
                            jnp.logical_and(place[axis] <= at[axis], at[axis] < grid[axis] - 1),
                            strides[axis],
                        ),
                        (
                            jnp.logical_and(place[axis] >= at[axis], at[axis] > 0),
                            -strides[axis],
                        ),
                    ]
                for condition, shift in options:
                    if clear is not None:
                        condition = jnp.logical_and(condition, clear)

                    @pl.when(condition)
                    def _(link=link, part=part, shift=shift):
                        act(part_copy(source, slot, link, part, chip + shift))

                    link += 1
        return source

    def stat_copy(source, half):
        return pltpu.make_async_remote_copy(
            src_ref=stat_out.at[source * 2 + half],
            dst_ref=stat_in.at[me],
            send_sem=stat_send,
            recv_sem=stat_recv,
            device_id=(half, source),
            device_id_type=MESH,
        )

    def score(source):
        block = xbuf[source].reshape(2 * xbuf.shape[2], xbuf.shape[3])
        products = lax.dot_general(
            copies[...], block, (((1,), (1,)), ((), ())), preferred_element_type=jnp.float32
        )
        scores = products * (2.0 * alpha) - norms[...]
        largest = jnp.max(scores, axis=0, keepdims=True)
        terms = jnp.exp2(scores - largest)
        ebuf[source] = terms
        summed = jnp.sum(terms, axis=0, keepdims=True)
        local_max[source] = largest
        half_width = block.shape[0] // 2
        for half in range(2):
            columns = slice(half * half_width, (half + 1) * half_width)
            stat_out[source * 2 + half] = jnp.concatenate(
                [largest[:, columns], summed[:, columns]], axis=0
            )
            mine = jnp.logical_and(source == chip, core == half)

            @pl.when(mine)
            def _(columns=columns):
                stat_in[me] = jnp.concatenate([largest[:, columns], summed[:, columns]], axis=0)

            @pl.when(jnp.logical_not(mine))
            def _(half=half):
                stat_copy(source, half).start()

    def run_step(step, carry):
        @pl.when(step < chips)
        def _():
            source = index_of(source_of(step, at, grid))

            @pl.when(step > 0)
            def _():
                for part in range(len(parts)):
                    part_copy(source, 0, 0, part, chip).wait_recv()

            if chips > SEND_DEPTH:

                @pl.when(step >= SEND_DEPTH)
                def _():
                    forwards(step - SEND_DEPTH, lambda copy: copy.wait_send())

            forwards(step, lambda copy: copy.start())
            side_copy(source).start()

        @pl.when(step == 0)
        def _():
            load.wait()
            values = acc[...].astype(jnp.bfloat16)
            copies[...] = values
            wide = values.astype(jnp.float32)
            squares = jnp.sum(wide * wide, axis=1, keepdims=True) * alpha
            norms[...] = jnp.broadcast_to(squares, norms.shape)

        @pl.when(step > 0)
        def _():
            source = index_of(source_of(step - 1, at, grid))
            side_copy(source).wait_recv()
            score(source)

        return carry

    lax.fori_loop(0, chips + 1, run_step, 0)

    everyone = pl.ds(0, devices - 1)
    pltpu.make_async_copy(stat_in.at[everyone], stat_in.at[everyone], stat_recv).wait()
    maxima = stat_in[:, 0, :]
    sums = stat_in[:, 1, :]
    largest = jnp.max(maxima, axis=0, keepdims=True)
    summed = jnp.sum(sums * jnp.exp2(maxima - largest), axis=0, keepdims=True)
    own_total = largest + jnp.log(summed) * LOG2E
    totals[me] = own_total
    total_ref[...] = own_total * LN2

    def tell(index, carry):
        other = lax.rem(me + index, devices)
        pltpu.make_async_remote_copy(
            src_ref=totals.at[me],
            dst_ref=totals.at[me],
            send_sem=total_send,
            recv_sem=total_recv,
            device_id=(lax.rem(other, 2), other // 2),
            device_id_type=MESH,
        ).start()
        return carry

    lax.fori_loop(1, devices, tell, 0)
    counts[...] = jnp.zeros_like(counts)
    pltpu.make_async_copy(totals.at[everyone], totals.at[everyone], total_recv).wait()

    width = 2 * xbuf.shape[2]

    def weigh(group, carry):
        for index in range(chunk):
            source = group * chunk + index
            total = jnp.concatenate([totals[source * 2], totals[source * 2 + 1]], axis=1)
            factor = jnp.exp2(local_max[source] - total)
            part = (ebuf[source] * factor).astype(jnp.bfloat16)
            weights[:, index * width : (index + 1) * width] = part
            wide = part.astype(jnp.float32)
            counts[...] += wide[:, : width // 2] + wide[:, width // 2 :]
        block = xbuf[pl.ds(group * chunk, chunk)].reshape(chunk * width, xbuf.shape[3])
        acc[...] += jnp.dot(weights[...], block, preferred_element_type=jnp.float32)
        return carry

    lax.fori_loop(0, chips // chunk, weigh, 0)

    tiles = 4
    span = own_rows // tiles
    stores = []
    for tile in range(tiles):
        rows = pl.ds(tile * span, span)
        scale = 1.0 / (jnp.sum(counts[rows, :], axis=1, keepdims=True) + 1.0)
        acc[rows, :] = acc[rows, :] * scale
        store = pltpu.make_async_copy(acc.at[rows], out_hbm.at[rows], store_sem.at[tile])
        store.start()
        stores.append(store)

    def settle(step, carry):
        forwards(step, lambda copy: copy.wait_send())
        source = index_of(source_of(step, at, grid))
        side_copy(source).wait_send()
        return carry

    lax.fori_loop(max(0, chips - SEND_DEPTH), chips, settle, 0)
    if chips > SEND_DEPTH:

        def settle_side(step, carry):
            side_copy(index_of(source_of(step, at, grid))).wait_send()
            return carry

        lax.fori_loop(0, chips - SEND_DEPTH, settle_side, 0)
    pltpu.make_async_copy(stat_out.at[everyone], stat_out.at[everyone], stat_send).wait()
    pltpu.make_async_copy(totals.at[everyone], totals.at[everyone], total_send).wait()
    for store in stores:
        store.wait()


def on_device(chips, points, centroids):
    rows, features = points.shape
    own = centroids.shape[0]
    grid = chip_grid(chips)
    parts = row_parts(rows)
    alpha = 7.0 / math.sqrt(features) * LOG2E
    devices = 2 * chips
    chunk = 4
    links = len(parts) * sum(0 if n == 1 else (1 if n == 2 else 2) for n in grid)
    dma = pltpu.SemaphoreType.DMA
    f32, bf16 = jnp.float32, jnp.bfloat16
    new_centroids, total = pl.pallas_call(
        functools.partial(kernel, grid, parts, alpha, chunk),
        out_shape=(
            jax.ShapeDtypeStruct((own, features), f32),
            jax.ShapeDtypeStruct((1, rows), f32),
        ),
        in_specs=[pl.BlockSpec(memory_space=pltpu.VMEM), pl.BlockSpec(memory_space=pl.ANY)],
        out_specs=(pl.BlockSpec(memory_space=pl.ANY), pl.BlockSpec(memory_space=pltpu.VMEM)),
        scratch_shapes=[
            pltpu.VMEM((chips, 2, rows, features), bf16),
            pltpu.VMEM((own, features), f32),
            pltpu.VMEM((own, features), bf16),
            pltpu.VMEM((own, 2 * rows), f32),
            pltpu.VMEM((chips, own, 2 * rows), f32),
            pltpu.VMEM((own, chunk * 2 * rows), bf16),
            pltpu.VMEM((own, rows), f32),
            pltpu.VMEM((chips, 1, 2 * rows), f32),
            pltpu.VMEM((devices, 2, rows), f32),
            pltpu.VMEM((devices, 2, rows), f32),
            pltpu.VMEM((devices, 1, rows), f32),
            dma,
            dma((4,)),
            dma((SEND_DEPTH, links)),
            dma((chips, len(parts))),
            dma((chips,)),
            dma((chips,)),
            dma,
            dma,
            dma,
            dma,
        ],
        compiler_params=pltpu.CompilerParams(
            collective_id=0, has_side_effects=True, vmem_limit_bytes=60 * 1024 * 1024
        ),
        cost_estimate=pl.CostEstimate(
            flops=4 * own * devices * rows * features,
            bytes_accessed=8 * own * features,
            transcendentals=own * devices * rows,
        ),
        name="refine",
    )(points, centroids)
    return (new_centroids, total.reshape(rows))


def solution(mesh):
    placed = (P(("dp", "cent"), None), P(("dp", "cent"), None))
    return jax.shard_map(
        functools.partial(on_device, mesh.shape["cent"]),
        mesh=mesh,
        in_specs=placed,
        out_specs=(P(("dp", "cent"), None), P(("dp", "cent"))),
        check_vma=False,
    )
```

```python
import functools
import math

import jax
import jax.numpy as jnp
from jax import lax
from jax.experimental import pallas as pl
from jax.experimental.pallas import tpu as pltpu
from jax.sharding import PartitionSpec as P

MESH = pl.DeviceIdType.MESH
LOG2E = 1.4426950408889634
LN2 = 0.6931471805599453
Z_AXIS, Y_AXIS, X_AXIS = 0, 1, 2
SHARES = (
    (0.375, (Z_AXIS, X_AXIS, Y_AXIS)),
    (0.375, (Z_AXIS, Y_AXIS, X_AXIS)),
    (0.125, (X_AXIS, Y_AXIS, Z_AXIS)),
    (0.125, (Y_AXIS, X_AXIS, Z_AXIS)),
)
SEND_DEPTH = 16
NEAREST = (
    (0, 0, 0), (1, 0, 0), (0, 0, 1), (0, 1, 0), (2, 0, 0), (0, 1, 1), (1, 0, 1), (1, 1, 0),
    (3, 0, 0), (1, 1, 1), (2, 0, 1), (2, 1, 0), (2, 1, 1), (3, 0, 1), (3, 1, 0), (3, 1, 1),
)


def chip_grid(chips):
    sizes = [1, 1, 1]
    axis = 0
    order = (Z_AXIS, Y_AXIS, X_AXIS)
    left = chips
    if chips >= 16:
        sizes[0] = 4
        left //= 4
    while left > 1:
        sizes[order[axis % 3]] *= 2 if (chips < 16 or axis % 3) else 1
        left = chips // (sizes[0] * sizes[1] * sizes[2])
        axis += 1
    return tuple(sizes)


def row_parts(rows):
    parts, first = [], 0
    for index, (share, order) in enumerate(SHARES):
        last = rows if index == len(SHARES) - 1 else first + int(share * rows) // 16 * 16
        parts.append((first, last - first, order))
        first = last
    return parts


def ranked(rank, at, size):
    if size == 1:
        return at * 0
    if size == 2:
        return lax.rem(at + rank, 2)
    low = jnp.where(at < 2, at, 3 - at)
    place = jnp.where(low == 0, rank, jnp.where(rank == 3, 3, lax.rem(rank + 1, 3)))
    return jnp.where(at < 2, place, 3 - place)


def source_of(step, at, grid):
    nz, ny, nx = grid
    if grid == (4, 2, 2):
        ranks = []
        for axis in range(3):
            value = jnp.int32(NEAREST[0][axis])
            for index in range(1, len(NEAREST)):
                value = jnp.where(step == index, NEAREST[index][axis], value)
            ranks.append(value)
    else:
        ranks = [step // (ny * nx), (step // nx) % ny, step % nx]
    return [ranked(rank, place, size) for rank, place, size in zip(ranks, at, grid)]


def kernel(
    grid, parts, alpha, chunk,
    points_ref, cent_hbm, out_hbm, total_ref,
    xbuf, acc, copies, norms, ebuf, weights, counts, local_max,
    stat_out, stat_in, totals,
    load_sem, store_sem, send_sem, recv_sem, side_send, side_recv,
    stat_send, stat_recv, total_send, total_recv,
):
    nz, ny, nx = grid
    chips = nz * ny * nx
    devices = 2 * chips
    core = lax.axis_index("dp")
    chip = lax.axis_index("cent")
    me = chip * 2 + core
    at = [chip // (ny * nx), (chip // nx) % ny, chip % nx]
    strides = (ny * nx, nx, 1)
    own_rows = copies.shape[0]

    load = pltpu.make_async_copy(cent_hbm, acc, load_sem)
    load.start()

    barrier = pltpu.get_barrier_semaphore()

    def greet(index, carry):
        other = lax.rem(me + index, devices)
        pl.semaphore_signal(
            barrier, inc=1, device_id=(lax.rem(other, 2), other // 2), device_id_type=MESH
        )
        return carry

    lax.fori_loop(1, devices, greet, 0)
    xbuf[chip, core] = points_ref[...]
    pl.semaphore_wait(barrier, devices - 1)

    def part_copy(source, slot, link, part, target):
        first, rows, _ = parts[part]
        piece = xbuf.at[source, core, pl.ds(first, rows)]
        return pltpu.make_async_remote_copy(
            src_ref=piece,
            dst_ref=piece,
            send_sem=send_sem.at[slot, link],
            recv_sem=recv_sem.at[source, part],
            device_id=(core, target),
            device_id_type=MESH,
        )

    def side_copy(source):
        return pltpu.make_async_remote_copy(
            src_ref=xbuf.at[source, core],
            dst_ref=xbuf.at[source, core],
            send_sem=side_send.at[source],
            recv_sem=side_recv.at[source],
            device_id=(1 - core, chip),
            device_id_type=MESH,
        )

    def index_of(place):
        return place[0] * strides[0] + place[1] * strides[1] + place[2]

    def forwards(step, act, ready=None):
        place = source_of(step, at, grid)
        source = index_of(place)
        slot = lax.rem(step, SEND_DEPTH)
        link = 0
        for part, (_, _, order) in enumerate(parts):
            if ready is not None:
                ready(source, part)
            for position, axis in enumerate(order):
                if grid[axis] == 1:
                    continue
                clear = None
                for later in order[position + 1 :]:
                    if grid[later] > 1:
                        same = place[later] == at[later]
                        clear = same if clear is None else jnp.logical_and(clear, same)
                if grid[axis] == 2:
                    options = [(place[axis] == at[axis], (1 - 2 * at[axis]) * strides[axis])]
                else:
                    options = [
                        (
                            jnp.logical_and(place[axis] <= at[axis], at[axis] < grid[axis] - 1),
                            strides[axis],
                        ),
                        (
                            jnp.logical_and(place[axis] >= at[axis], at[axis] > 0),
                            -strides[axis],
                        ),
                    ]
                for condition, shift in options:
                    if clear is not None:
                        condition = jnp.logical_and(condition, clear)

                    @pl.when(condition)
                    def _(link=link, part=part, shift=shift):
                        act(part_copy(source, slot, link, part, chip + shift))

                    link += 1
        return source

    def stat_copy(source, half):
        return pltpu.make_async_remote_copy(
            src_ref=stat_out.at[source * 2 + half],
            dst_ref=stat_in.at[me],
            send_sem=stat_send,
            recv_sem=stat_recv,
            device_id=(half, source),
            device_id_type=MESH,
        )

    def score(source):
        block = xbuf[source].reshape(2 * xbuf.shape[2], xbuf.shape[3])
        products = lax.dot_general(
            copies[...], block, (((1,), (1,)), ((), ())), preferred_element_type=jnp.float32
        )
        scores = products * (2.0 * alpha) - norms[...]
        largest = jnp.max(scores, axis=0, keepdims=True)
        terms = jnp.exp2(scores - largest)
        ebuf[source] = terms
        summed = jnp.sum(terms, axis=0, keepdims=True)
        local_max[source] = largest
        half_width = block.shape[0] // 2
        for half in range(2):
            columns = slice(half * half_width, (half + 1) * half_width)
            stat_out[source * 2 + half] = jnp.concatenate(
                [largest[:, columns], summed[:, columns]], axis=0
            )
            mine = jnp.logical_and(source == chip, core == half)

            @pl.when(mine)
            def _(columns=columns):
                stat_in[me] = jnp.concatenate([largest[:, columns], summed[:, columns]], axis=0)

            @pl.when(jnp.logical_not(mine))
            def _(half=half):
                stat_copy(source, half).start()

    def run_step(step, carry):
        @pl.when(step < chips)
        def _():
            source = index_of(source_of(step, at, grid))

            def ready(source, part):
                @pl.when(step > 0)
                def _():
                    part_copy(source, 0, 0, part, chip).wait_recv()

            if chips > SEND_DEPTH:

                @pl.when(step >= SEND_DEPTH)
                def _():
                    forwards(step - SEND_DEPTH, lambda copy: copy.wait_send())

            forwards(step, lambda copy: copy.start(), ready)
            side_copy(source).start()

        @pl.when(step == 0)
        def _():
            load.wait()
            values = acc[...].astype(jnp.bfloat16)
            copies[...] = values
            wide = values.astype(jnp.float32)
            squares = jnp.sum(wide * wide, axis=1, keepdims=True) * alpha
            norms[...] = jnp.broadcast_to(squares, norms.shape)

        @pl.when(step > 0)
        def _():
            source = index_of(source_of(step - 1, at, grid))
            side_copy(source).wait_recv()
            score(source)

        return carry

    lax.fori_loop(0, chips + 1, run_step, 0)

    everyone = pl.ds(0, devices - 1)
    pltpu.make_async_copy(stat_in.at[everyone], stat_in.at[everyone], stat_recv).wait()
    maxima = stat_in[:, 0, :]
    sums = stat_in[:, 1, :]
    largest = jnp.max(maxima, axis=0, keepdims=True)
    summed = jnp.sum(sums * jnp.exp2(maxima - largest), axis=0, keepdims=True)
    own_total = largest + jnp.log(summed) * LOG2E
    totals[me] = own_total
    total_ref[...] = own_total * LN2

    def tell(index, carry):
        other = lax.rem(me + index, devices)
        pltpu.make_async_remote_copy(
            src_ref=totals.at[me],
            dst_ref=totals.at[me],
            send_sem=total_send,
            recv_sem=total_recv,
            device_id=(lax.rem(other, 2), other // 2),
            device_id_type=MESH,
        ).start()
        return carry

    lax.fori_loop(1, devices, tell, 0)
    counts[...] = jnp.zeros_like(counts)
    pltpu.make_async_copy(totals.at[everyone], totals.at[everyone], total_recv).wait()

    width = 2 * xbuf.shape[2]

    def weigh(group, carry):
        for index in range(chunk):
            source = group * chunk + index
            total = jnp.concatenate([totals[source * 2], totals[source * 2 + 1]], axis=1)
            factor = jnp.exp2(local_max[source] - total)
            part = (ebuf[source] * factor).astype(jnp.bfloat16)
            weights[:, index * width : (index + 1) * width] = part
            wide = part.astype(jnp.float32)
            counts[...] += wide[:, : width // 2] + wide[:, width // 2 :]
        block = xbuf[pl.ds(group * chunk, chunk)].reshape(chunk * width, xbuf.shape[3])
        acc[...] += jnp.dot(weights[...], block, preferred_element_type=jnp.float32)
        return carry

    lax.fori_loop(0, chips // chunk, weigh, 0)

    tiles = 4
    span = own_rows // tiles
    stores = []
    for tile in range(tiles):
        rows = pl.ds(tile * span, span)
        scale = 1.0 / (jnp.sum(counts[rows, :], axis=1, keepdims=True) + 1.0)
        acc[rows, :] = acc[rows, :] * scale
        store = pltpu.make_async_copy(acc.at[rows], out_hbm.at[rows], store_sem.at[tile])
        store.start()
        stores.append(store)

    def settle(step, carry):
        forwards(step, lambda copy: copy.wait_send())
        source = index_of(source_of(step, at, grid))
        side_copy(source).wait_send()
        return carry

    lax.fori_loop(max(0, chips - SEND_DEPTH), chips, settle, 0)
    if chips > SEND_DEPTH:

        def settle_side(step, carry):
            side_copy(index_of(source_of(step, at, grid))).wait_send()
            return carry

        lax.fori_loop(0, chips - SEND_DEPTH, settle_side, 0)
    pltpu.make_async_copy(stat_out.at[everyone], stat_out.at[everyone], stat_send).wait()
    pltpu.make_async_copy(totals.at[everyone], totals.at[everyone], total_send).wait()
    for store in stores:
        store.wait()


def on_device(chips, points, centroids):
    rows, features = points.shape
    own = centroids.shape[0]
    grid = chip_grid(chips)
    parts = row_parts(rows)
    alpha = 7.0 / math.sqrt(features) * LOG2E
    devices = 2 * chips
    chunk = 4
    links = len(parts) * sum(0 if n == 1 else (1 if n == 2 else 2) for n in grid)
    dma = pltpu.SemaphoreType.DMA
    f32, bf16 = jnp.float32, jnp.bfloat16
    new_centroids, total = pl.pallas_call(
        functools.partial(kernel, grid, parts, alpha, chunk),
        out_shape=(
            jax.ShapeDtypeStruct((own, features), f32),
            jax.ShapeDtypeStruct((1, rows), f32),
        ),
        in_specs=[pl.BlockSpec(memory_space=pltpu.VMEM), pl.BlockSpec(memory_space=pl.ANY)],
        out_specs=(pl.BlockSpec(memory_space=pl.ANY), pl.BlockSpec(memory_space=pltpu.VMEM)),
        scratch_shapes=[
            pltpu.VMEM((chips, 2, rows, features), bf16),
            pltpu.VMEM((own, features), f32),
            pltpu.VMEM((own, features), bf16),
            pltpu.VMEM((own, 2 * rows), f32),
            pltpu.VMEM((chips, own, 2 * rows), f32),
            pltpu.VMEM((own, chunk * 2 * rows), bf16),
            pltpu.VMEM((own, rows), f32),
            pltpu.VMEM((chips, 1, 2 * rows), f32),
            pltpu.VMEM((devices, 2, rows), f32),
            pltpu.VMEM((devices, 2, rows), f32),
            pltpu.VMEM((devices, 1, rows), f32),
            dma,
            dma((4,)),
            dma((SEND_DEPTH, links)),
            dma((chips, len(parts))),
            dma((chips,)),
            dma((chips,)),
            dma,
            dma,
            dma,
            dma,
        ],
        compiler_params=pltpu.CompilerParams(
            collective_id=0, has_side_effects=True, vmem_limit_bytes=60 * 1024 * 1024
        ),
        cost_estimate=pl.CostEstimate(
            flops=4 * own * devices * rows * features,
            bytes_accessed=8 * own * features,
            transcendentals=own * devices * rows,
        ),
        name="refine",
    )(points, centroids)
    return (new_centroids, total.reshape(rows))


def solution(mesh):
    placed = (P(("dp", "cent"), None), P(("dp", "cent"), None))
    return jax.shard_map(
        functools.partial(on_device, mesh.shape["cent"]),
        mesh=mesh,
        in_specs=placed,
        out_specs=(P(("dp", "cent"), None), P(("dp", "cent"))),
        check_vma=False,
    )
```

```python
import functools
import math

import jax
import jax.numpy as jnp
from jax import lax
from jax.experimental import pallas as pl
from jax.experimental.pallas import tpu as pltpu
from jax.sharding import PartitionSpec as P

MESH = pl.DeviceIdType.MESH
LOG2E = 1.4426950408889634
LN2 = 0.6931471805599453
Z_AXIS, Y_AXIS, X_AXIS = 0, 1, 2
SHARES = (
    (0.375, (Z_AXIS, X_AXIS, Y_AXIS)),
    (0.375, (Z_AXIS, Y_AXIS, X_AXIS)),
    (0.125, (X_AXIS, Y_AXIS, Z_AXIS)),
    (0.125, (Y_AXIS, X_AXIS, Z_AXIS)),
)
SEND_DEPTH = 16
NEAREST = (
    (0, 0, 0), (1, 0, 0), (0, 0, 1), (0, 1, 0), (2, 0, 0), (0, 1, 1), (1, 0, 1), (1, 1, 0),
    (3, 0, 0), (1, 1, 1), (2, 0, 1), (2, 1, 0), (2, 1, 1), (3, 0, 1), (3, 1, 0), (3, 1, 1),
)


def chip_grid(chips):
    sizes = [1, 1, 1]
    axis = 0
    order = (Z_AXIS, Y_AXIS, X_AXIS)
    left = chips
    if chips >= 16:
        sizes[0] = 4
        left //= 4
    while left > 1:
        sizes[order[axis % 3]] *= 2 if (chips < 16 or axis % 3) else 1
        left = chips // (sizes[0] * sizes[1] * sizes[2])
        axis += 1
    return tuple(sizes)


def row_parts(rows):
    parts, first = [], 0
    for index, (share, order) in enumerate(SHARES):
        last = rows if index == len(SHARES) - 1 else first + int(share * rows) // 16 * 16
        parts.append((first, last - first, order))
        first = last
    return parts


def ranked(rank, at, size):
    if size == 1:
        return at * 0
    if size == 2:
        return lax.rem(at + rank, 2)
    low = jnp.where(at < 2, at, 3 - at)
    place = jnp.where(low == 0, rank, jnp.where(rank == 3, 3, lax.rem(rank + 1, 3)))
    return jnp.where(at < 2, place, 3 - place)


def source_of(step, at, grid):
    nz, ny, nx = grid
    if grid == (4, 2, 2):
        ranks = []
        for axis in range(3):
            value = jnp.int32(NEAREST[0][axis])
            for index in range(1, len(NEAREST)):
                value = jnp.where(step == index, NEAREST[index][axis], value)
            ranks.append(value)
    else:
        ranks = [step // (ny * nx), (step // nx) % ny, step % nx]
    return [ranked(rank, place, size) for rank, place, size in zip(ranks, at, grid)]


def kernel(
    grid, parts, alpha, chunk,
    points_ref, cent_hbm, acc, total_ref,
    xbuf, copies, norms, ebuf, weights, counts, local_max,
    stat_out, stat_in, totals,
    load_sem, send_sem, recv_sem, side_send, side_recv,
    stat_send, stat_recv, total_send, total_recv,
):
    nz, ny, nx = grid
    chips = nz * ny * nx
    devices = 2 * chips
    core = lax.axis_index("dp")
    chip = lax.axis_index("cent")
    me = chip * 2 + core
    at = [chip // (ny * nx), (chip // nx) % ny, chip % nx]
    strides = (ny * nx, nx, 1)
    own_rows = copies.shape[0]

    own_block = pltpu.make_async_copy(points_ref, xbuf.at[chip, core], load_sem.at[0])
    own_block.start()
    load = pltpu.make_async_copy(cent_hbm, acc, load_sem.at[1])
    load.start()

    barrier = pltpu.get_barrier_semaphore()

    def greet(index, carry):
        other = lax.rem(me + index, devices)
        pl.semaphore_signal(
            barrier, inc=1, device_id=(lax.rem(other, 2), other // 2), device_id_type=MESH
        )
        return carry

    lax.fori_loop(1, devices, greet, 0)
    own_block.wait()
    pl.semaphore_wait(barrier, devices - 1)

    def part_copy(source, slot, link, part, target):
        first, rows, _ = parts[part]
        piece = xbuf.at[source, core, pl.ds(first, rows)]
        return pltpu.make_async_remote_copy(
            src_ref=piece,
            dst_ref=piece,
            send_sem=send_sem.at[slot, link],
            recv_sem=recv_sem.at[source, part],
            device_id=(core, target),
            device_id_type=MESH,
        )

    def side_copy(source):
        return pltpu.make_async_remote_copy(
            src_ref=xbuf.at[source, core],
            dst_ref=xbuf.at[source, core],
            send_sem=side_send.at[source],
            recv_sem=side_recv.at[source],
            device_id=(1 - core, chip),
            device_id_type=MESH,
        )

    def index_of(place):
        return place[0] * strides[0] + place[1] * strides[1] + place[2]

    def forwards(step, act, ready=None):
        place = source_of(step, at, grid)
        source = index_of(place)
        slot = lax.rem(step, SEND_DEPTH)
        link = 0
        for part, (_, _, order) in enumerate(parts):
            if ready is not None:
                ready(source, part)
            for position, axis in enumerate(order):
                if grid[axis] == 1:
                    continue
                clear = None
                for later in order[position + 1 :]:
                    if grid[later] > 1:
                        same = place[later] == at[later]
                        clear = same if clear is None else jnp.logical_and(clear, same)
                if grid[axis] == 2:
                    options = [(place[axis] == at[axis], (1 - 2 * at[axis]) * strides[axis])]
                else:
                    options = [
                        (
                            jnp.logical_and(place[axis] <= at[axis], at[axis] < grid[axis] - 1),
                            strides[axis],
                        ),
                        (
                            jnp.logical_and(place[axis] >= at[axis], at[axis] > 0),
                            -strides[axis],
                        ),
                    ]
                for condition, shift in options:
                    if clear is not None:
                        condition = jnp.logical_and(condition, clear)

                    @pl.when(condition)
                    def _(link=link, part=part, shift=shift):
                        act(part_copy(source, slot, link, part, chip + shift))

                    link += 1
        return source

    def stat_copy(source, half):
        return pltpu.make_async_remote_copy(
            src_ref=stat_out.at[source * 2 + half],
            dst_ref=stat_in.at[me],
            send_sem=stat_send,
            recv_sem=stat_recv,
            device_id=(half, source),
            device_id_type=MESH,
        )

    def score(source):
        block = xbuf[source].reshape(2 * xbuf.shape[2], xbuf.shape[3])
        products = lax.dot_general(
            copies[...], block, (((1,), (1,)), ((), ())), preferred_element_type=jnp.float32
        )
        scores = products * (2.0 * alpha) - norms[...]
        largest = jnp.max(scores, axis=0, keepdims=True)
        terms = jnp.exp2(scores - largest)
        ebuf[source] = terms
        summed = jnp.sum(terms, axis=0, keepdims=True)
        local_max[source] = largest
        half_width = block.shape[0] // 2
        for half in range(2):
            columns = slice(half * half_width, (half + 1) * half_width)
            stat_out[source * 2 + half] = jnp.concatenate(
                [largest[:, columns], summed[:, columns]], axis=0
            )
            mine = jnp.logical_and(source == chip, core == half)

            @pl.when(mine)
            def _(columns=columns):
                stat_in[me] = jnp.concatenate([largest[:, columns], summed[:, columns]], axis=0)

            @pl.when(jnp.logical_not(mine))
            def _(half=half):
                stat_copy(source, half).start()

    def run_step(step, carry):
        @pl.when(step < chips)
        def _():
            source = index_of(source_of(step, at, grid))

            def ready(source, part):
                @pl.when(step > 0)
                def _():
                    part_copy(source, 0, 0, part, chip).wait_recv()

            if chips > SEND_DEPTH:

                @pl.when(step >= SEND_DEPTH)
                def _():
                    forwards(step - SEND_DEPTH, lambda copy: copy.wait_send())

            forwards(step, lambda copy: copy.start(), ready)
            side_copy(source).start()

        @pl.when(step == 0)
        def _():
            load.wait()
            values = acc[...].astype(jnp.bfloat16)
            copies[...] = values
            wide = values.astype(jnp.float32)
            squares = jnp.sum(wide * wide, axis=1, keepdims=True) * alpha
            norms[...] = jnp.broadcast_to(squares, norms.shape)

        @pl.when(step > 0)
        def _():
            source = index_of(source_of(step - 1, at, grid))
            side_copy(source).wait_recv()
            score(source)

        return carry

    lax.fori_loop(0, chips + 1, run_step, 0)

    everyone = pl.ds(0, devices - 1)
    pltpu.make_async_copy(stat_in.at[everyone], stat_in.at[everyone], stat_recv).wait()
    maxima = stat_in[:, 0, :]
    sums = stat_in[:, 1, :]
    largest = jnp.max(maxima, axis=0, keepdims=True)
    summed = jnp.sum(sums * jnp.exp2(maxima - largest), axis=0, keepdims=True)
    own_total = largest + jnp.log(summed) * LOG2E
    totals[me] = own_total
    total_ref[...] = own_total * LN2

    def tell(index, carry):
        other = lax.rem(me + index, devices)
        pltpu.make_async_remote_copy(
            src_ref=totals.at[me],
            dst_ref=totals.at[me],
            send_sem=total_send,
            recv_sem=total_recv,
            device_id=(lax.rem(other, 2), other // 2),
            device_id_type=MESH,
        ).start()
        return carry

    lax.fori_loop(1, devices, tell, 0)
    counts[...] = jnp.zeros_like(counts)
    pltpu.make_async_copy(totals.at[everyone], totals.at[everyone], total_recv).wait()

    width = 2 * xbuf.shape[2]

    def weigh(group, carry):
        for index in range(chunk):
            source = group * chunk + index
            total = jnp.concatenate([totals[source * 2], totals[source * 2 + 1]], axis=1)
            factor = jnp.exp2(local_max[source] - total)
            part = (ebuf[source] * factor).astype(jnp.bfloat16)
            weights[:, index * width : (index + 1) * width] = part
            wide = part.astype(jnp.float32)
            counts[...] += wide[:, : width // 2] + wide[:, width // 2 :]
        block = xbuf[pl.ds(group * chunk, chunk)].reshape(chunk * width, xbuf.shape[3])
        acc[...] += jnp.dot(weights[...], block, preferred_element_type=jnp.float32)
        return carry

    lax.fori_loop(0, chips // chunk, weigh, 0)

    tiles = 4
    span = own_rows // tiles
    for tile in range(tiles):
        rows = pl.ds(tile * span, span)
        scale = 1.0 / (jnp.sum(counts[rows, :], axis=1, keepdims=True) + 1.0)
        acc[rows, :] = acc[rows, :] * scale

    def settle(step, carry):
        forwards(step, lambda copy: copy.wait_send())
        source = index_of(source_of(step, at, grid))
        side_copy(source).wait_send()
        return carry

    lax.fori_loop(max(0, chips - SEND_DEPTH), chips, settle, 0)
    if chips > SEND_DEPTH:

        def settle_side(step, carry):
            side_copy(index_of(source_of(step, at, grid))).wait_send()
            return carry

        lax.fori_loop(0, chips - SEND_DEPTH, settle_side, 0)
    pltpu.make_async_copy(stat_out.at[everyone], stat_out.at[everyone], stat_send).wait()
    pltpu.make_async_copy(totals.at[everyone], totals.at[everyone], total_send).wait()


def on_device(chips, points, centroids):
    rows, features = points.shape
    own = centroids.shape[0]
    grid = chip_grid(chips)
    parts = row_parts(rows)
    alpha = 7.0 / math.sqrt(features) * LOG2E
    devices = 2 * chips
    chunk = 4
    links = len(parts) * sum(0 if n == 1 else (1 if n == 2 else 2) for n in grid)
    dma = pltpu.SemaphoreType.DMA
    f32, bf16 = jnp.float32, jnp.bfloat16
    new_centroids, total = pl.pallas_call(
        functools.partial(kernel, grid, parts, alpha, chunk),
        out_shape=(
            jax.ShapeDtypeStruct((own, features), f32),
            jax.ShapeDtypeStruct((1, rows), f32),
        ),
        in_specs=[pl.BlockSpec(memory_space=pltpu.HBM), pl.BlockSpec(memory_space=pltpu.HBM)],
        out_specs=(pl.BlockSpec(memory_space=pltpu.VMEM), pl.BlockSpec(memory_space=pltpu.VMEM)),
        scratch_shapes=[
            pltpu.VMEM((chips, 2, rows, features), bf16),
            pltpu.VMEM((own, features), bf16),
            pltpu.VMEM((own, 2 * rows), f32),
            pltpu.VMEM((chips, own, 2 * rows), f32),
            pltpu.VMEM((own, chunk * 2 * rows), bf16),
            pltpu.VMEM((own, rows), f32),
            pltpu.VMEM((chips, 1, 2 * rows), f32),
            pltpu.VMEM((devices, 2, rows), f32),
            pltpu.VMEM((devices, 2, rows), f32),
            pltpu.VMEM((devices, 1, rows), f32),
            dma((2,)),
            dma((SEND_DEPTH, links)),
            dma((chips, len(parts))),
            dma((chips,)),
            dma((chips,)),
            dma,
            dma,
            dma,
            dma,
        ],
        compiler_params=pltpu.CompilerParams(
            collective_id=0, has_side_effects=True, vmem_limit_bytes=48 * 1024 * 1024
        ),
        cost_estimate=pl.CostEstimate(
            flops=4 * own * devices * rows * features,
            bytes_accessed=8 * own * features,
            transcendentals=own * devices * rows,
        ),
        name="refine",
    )(points, centroids)
    return (new_centroids, total.reshape(rows))


def solution(mesh):
    placed = (P(("dp", "cent"), None), P(("dp", "cent"), None))
    return jax.shard_map(
        functools.partial(on_device, mesh.shape["cent"]),
        mesh=mesh,
        in_specs=placed,
        out_specs=(P(("dp", "cent"), None), P(("dp", "cent"))),
        check_vma=False,
    )
```

```python
import functools
import math

import jax
import jax.numpy as jnp
from jax import lax
from jax.experimental import pallas as pl
from jax.experimental.pallas import tpu as pltpu
from jax.sharding import PartitionSpec as P

MESH = pl.DeviceIdType.MESH
LOG2E = 1.4426950408889634
LN2 = 0.6931471805599453
Z_AXIS, Y_AXIS, X_AXIS = 0, 1, 2
SHARES = (
    (0.5, (Z_AXIS, X_AXIS, Y_AXIS)),
    (0.5, (Z_AXIS, Y_AXIS, X_AXIS)),
)
SEND_DEPTH = 16
NEAREST = (
    (0, 0, 0), (1, 0, 0), (0, 0, 1), (0, 1, 0), (2, 0, 0), (0, 1, 1), (1, 0, 1), (1, 1, 0),
    (3, 0, 0), (1, 1, 1), (2, 0, 1), (2, 1, 0), (2, 1, 1), (3, 0, 1), (3, 1, 0), (3, 1, 1),
)


def chip_grid(chips):
    sizes = [1, 1, 1]
    axis = 0
    order = (Z_AXIS, Y_AXIS, X_AXIS)
    left = chips
    if chips >= 16:
        sizes[0] = 4
        left //= 4
    while left > 1:
        sizes[order[axis % 3]] *= 2 if (chips < 16 or axis % 3) else 1
        left = chips // (sizes[0] * sizes[1] * sizes[2])
        axis += 1
    return tuple(sizes)


def row_parts(rows):
    parts, first = [], 0
    for index, (share, order) in enumerate(SHARES):
        last = rows if index == len(SHARES) - 1 else first + int(share * rows) // 16 * 16
        parts.append((first, last - first, order))
        first = last
    return parts


def ranked(rank, at, size):
    if size == 1:
        return at * 0
    if size == 2:
        return lax.rem(at + rank, 2)
    low = jnp.where(at < 2, at, 3 - at)
    place = jnp.where(low == 0, rank, jnp.where(rank == 3, 3, lax.rem(rank + 1, 3)))
    return jnp.where(at < 2, place, 3 - place)


def source_of(step, at, grid):
    nz, ny, nx = grid
    if grid == (4, 2, 2):
        ranks = []
        for axis in range(3):
            value = jnp.int32(NEAREST[0][axis])
            for index in range(1, len(NEAREST)):
                value = jnp.where(step == index, NEAREST[index][axis], value)
            ranks.append(value)
    else:
        ranks = [step // (ny * nx), (step // nx) % ny, step % nx]
    return [ranked(rank, place, size) for rank, place, size in zip(ranks, at, grid)]


def kernel(
    grid, parts, alpha, chunk,
    points_ref, cent_hbm, acc, total_ref,
    xbuf, copies, norms, ebuf, weights, counts, local_max,
    stat_out, stat_in, totals,
    load_sem, send_sem, recv_sem, side_send, side_recv,
    stat_send, stat_recv, total_send, total_recv,
):
    nz, ny, nx = grid
    chips = nz * ny * nx
    devices = 2 * chips
    core = lax.axis_index("dp")
    chip = lax.axis_index("cent")
    me = chip * 2 + core
    at = [chip // (ny * nx), (chip // nx) % ny, chip % nx]
    strides = (ny * nx, nx, 1)
    own_rows = copies.shape[0]

    own_block = pltpu.make_async_copy(points_ref, xbuf.at[chip, core], load_sem.at[0])
    own_block.start()
    load = pltpu.make_async_copy(cent_hbm, acc, load_sem.at[1])
    load.start()

    barrier = pltpu.get_barrier_semaphore()

    def greet(index, carry):
        other = lax.rem(me + index, devices)
        pl.semaphore_signal(
            barrier, inc=1, device_id=(lax.rem(other, 2), other // 2), device_id_type=MESH
        )
        return carry

    lax.fori_loop(1, devices, greet, 0)
    own_block.wait()
    pl.semaphore_wait(barrier, devices - 1)

    def part_copy(source, slot, link, part, target):
        first, rows, _ = parts[part]
        piece = xbuf.at[source, core, pl.ds(first, rows)]
        return pltpu.make_async_remote_copy(
            src_ref=piece,
            dst_ref=piece,
            send_sem=send_sem.at[slot, link],
            recv_sem=recv_sem.at[source, part],
            device_id=(core, target),
            device_id_type=MESH,
        )

    def side_copy(source):
        return pltpu.make_async_remote_copy(
            src_ref=xbuf.at[source, core],
            dst_ref=xbuf.at[source, core],
            send_sem=side_send.at[source],
            recv_sem=side_recv.at[source],
            device_id=(1 - core, chip),
            device_id_type=MESH,
        )

    def index_of(place):
        return place[0] * strides[0] + place[1] * strides[1] + place[2]

    def forwards(step, act, ready=None):
        place = source_of(step, at, grid)
        source = index_of(place)
        slot = lax.rem(step, SEND_DEPTH)
        link = 0
        for part, (_, _, order) in enumerate(parts):
            if ready is not None:
                ready(source, part)
            for position, axis in enumerate(order):
                if grid[axis] == 1:
                    continue
                clear = None
                for later in order[position + 1 :]:
                    if grid[later] > 1:
                        same = place[later] == at[later]
                        clear = same if clear is None else jnp.logical_and(clear, same)
                if grid[axis] == 2:
                    options = [(place[axis] == at[axis], (1 - 2 * at[axis]) * strides[axis])]
                else:
                    options = [
                        (
                            jnp.logical_and(place[axis] <= at[axis], at[axis] < grid[axis] - 1),
                            strides[axis],
                        ),
                        (
                            jnp.logical_and(place[axis] >= at[axis], at[axis] > 0),
                            -strides[axis],
                        ),
                    ]
                for condition, shift in options:
                    if clear is not None:
                        condition = jnp.logical_and(condition, clear)

                    @pl.when(condition)
                    def _(link=link, part=part, shift=shift):
                        act(part_copy(source, slot, link, part, chip + shift))

                    link += 1
        return source

    def stat_copy(source, half):
        return pltpu.make_async_remote_copy(
            src_ref=stat_out.at[source * 2 + half],
            dst_ref=stat_in.at[me],
            send_sem=stat_send,
            recv_sem=stat_recv,
            device_id=(half, source),
            device_id_type=MESH,
        )

    def score(source):
        block = xbuf[source].reshape(2 * xbuf.shape[2], xbuf.shape[3])
        products = lax.dot_general(
            copies[...], block, (((1,), (1,)), ((), ())), preferred_element_type=jnp.float32
        )
        scores = products * (2.0 * alpha) - norms[...]
        largest = jnp.max(scores, axis=0, keepdims=True)
        terms = jnp.exp2(scores - largest)
        ebuf[source] = terms
        summed = jnp.sum(terms, axis=0, keepdims=True)
        local_max[source] = largest
        half_width = block.shape[0] // 2
        for half in range(2):
            columns = slice(half * half_width, (half + 1) * half_width)
            stat_out[source * 2 + half] = jnp.concatenate(
                [largest[:, columns], summed[:, columns]], axis=0
            )
            mine = jnp.logical_and(source == chip, core == half)

            @pl.when(mine)
            def _(columns=columns):
                stat_in[me] = jnp.concatenate([largest[:, columns], summed[:, columns]], axis=0)

            @pl.when(jnp.logical_not(mine))
            def _(half=half):
                stat_copy(source, half).start()

    def run_step(step, carry):
        @pl.when(step < chips)
        def _():
            source = index_of(source_of(step, at, grid))

            def ready(source, part):
                @pl.when(step > 0)
                def _():
                    part_copy(source, 0, 0, part, chip).wait_recv()

            if chips > SEND_DEPTH:

                @pl.when(step >= SEND_DEPTH)
                def _():
                    forwards(step - SEND_DEPTH, lambda copy: copy.wait_send())

            forwards(step, lambda copy: copy.start(), ready)
            side_copy(source).start()

        @pl.when(step == 0)
        def _():
            load.wait()
            values = acc[...].astype(jnp.bfloat16)
            copies[...] = values
            wide = values.astype(jnp.float32)
            squares = jnp.sum(wide * wide, axis=1, keepdims=True) * alpha
            norms[...] = jnp.broadcast_to(squares, norms.shape)

        @pl.when(step > 1)
        def _():
            source = index_of(source_of(step - 2, at, grid))
            side_copy(source).wait_recv()
            score(source)

        return carry

    lax.fori_loop(0, chips + 2, run_step, 0)

    everyone = pl.ds(0, devices - 1)
    pltpu.make_async_copy(stat_in.at[everyone], stat_in.at[everyone], stat_recv).wait()
    maxima = stat_in[:, 0, :]
    sums = stat_in[:, 1, :]
    largest = jnp.max(maxima, axis=0, keepdims=True)
    summed = jnp.sum(sums * jnp.exp2(maxima - largest), axis=0, keepdims=True)
    own_total = largest + jnp.log(summed) * LOG2E
    totals[me] = own_total
    total_ref[...] = own_total * LN2

    def tell(index, carry):
        other = lax.rem(me + index, devices)
        pltpu.make_async_remote_copy(
            src_ref=totals.at[me],
            dst_ref=totals.at[me],
            send_sem=total_send,
            recv_sem=total_recv,
            device_id=(lax.rem(other, 2), other // 2),
            device_id_type=MESH,
        ).start()
        return carry

    lax.fori_loop(1, devices, tell, 0)
    counts[...] = jnp.zeros_like(counts)
    pltpu.make_async_copy(totals.at[everyone], totals.at[everyone], total_recv).wait()

    width = 2 * xbuf.shape[2]

    def weigh(group, carry):
        for index in range(chunk):
            source = group * chunk + index
            total = jnp.concatenate([totals[source * 2], totals[source * 2 + 1]], axis=1)
            factor = jnp.exp2(local_max[source] - total)
            part = (ebuf[source] * factor).astype(jnp.bfloat16)
            weights[:, index * width : (index + 1) * width] = part
            wide = part.astype(jnp.float32)
            counts[...] += wide[:, : width // 2] + wide[:, width // 2 :]
        block = xbuf[pl.ds(group * chunk, chunk)].reshape(chunk * width, xbuf.shape[3])
        acc[...] += jnp.dot(weights[...], block, preferred_element_type=jnp.float32)
        return carry

    lax.fori_loop(0, chips // chunk, weigh, 0)

    tiles = 4
    span = own_rows // tiles
    for tile in range(tiles):
        rows = pl.ds(tile * span, span)
        scale = 1.0 / (jnp.sum(counts[rows, :], axis=1, keepdims=True) + 1.0)
        acc[rows, :] = acc[rows, :] * scale

    def settle(step, carry):
        forwards(step, lambda copy: copy.wait_send())
        source = index_of(source_of(step, at, grid))
        side_copy(source).wait_send()
        return carry

    lax.fori_loop(max(0, chips - SEND_DEPTH), chips, settle, 0)
    if chips > SEND_DEPTH:

        def settle_side(step, carry):
            side_copy(index_of(source_of(step, at, grid))).wait_send()
            return carry

        lax.fori_loop(0, chips - SEND_DEPTH, settle_side, 0)
    pltpu.make_async_copy(stat_out.at[everyone], stat_out.at[everyone], stat_send).wait()
    pltpu.make_async_copy(totals.at[everyone], totals.at[everyone], total_send).wait()


def on_device(chips, points, centroids):
    rows, features = points.shape
    own = centroids.shape[0]
    grid = chip_grid(chips)
    parts = row_parts(rows)
    alpha = 7.0 / math.sqrt(features) * LOG2E
    devices = 2 * chips
    chunk = 8
    links = len(parts) * sum(0 if n == 1 else (1 if n == 2 else 2) for n in grid)
    dma = pltpu.SemaphoreType.DMA
    f32, bf16 = jnp.float32, jnp.bfloat16
    new_centroids, total = pl.pallas_call(
        functools.partial(kernel, grid, parts, alpha, chunk),
        out_shape=(
            jax.ShapeDtypeStruct((own, features), f32),
            jax.ShapeDtypeStruct((1, rows), f32),
        ),
        in_specs=[pl.BlockSpec(memory_space=pltpu.HBM), pl.BlockSpec(memory_space=pltpu.HBM)],
        out_specs=(pl.BlockSpec(memory_space=pltpu.VMEM), pl.BlockSpec(memory_space=pltpu.VMEM)),
        scratch_shapes=[
            pltpu.VMEM((chips, 2, rows, features), bf16),
            pltpu.VMEM((own, features), bf16),
            pltpu.VMEM((own, 2 * rows), f32),
            pltpu.VMEM((chips, own, 2 * rows), f32),
            pltpu.VMEM((own, chunk * 2 * rows), bf16),
            pltpu.VMEM((own, rows), f32),
            pltpu.VMEM((chips, 1, 2 * rows), f32),
            pltpu.VMEM((devices, 2, rows), f32),
            pltpu.VMEM((devices, 2, rows), f32),
            pltpu.VMEM((devices, 1, rows), f32),
            dma((2,)),
            dma((SEND_DEPTH, links)),
            dma((chips, len(parts))),
            dma((chips,)),
            dma((chips,)),
            dma,
            dma,
            dma,
            dma,
        ],
        compiler_params=pltpu.CompilerParams(
            collective_id=0, has_side_effects=True, vmem_limit_bytes=48 * 1024 * 1024
        ),
        cost_estimate=pl.CostEstimate(
            flops=4 * own * devices * rows * features,
            bytes_accessed=8 * own * features,
            transcendentals=own * devices * rows,
        ),
        name="refine",
    )(points, centroids)
    return (new_centroids, total.reshape(rows))


def solution(mesh):
    placed = (P(("dp", "cent"), None), P(("dp", "cent"), None))
    return jax.shard_map(
        functools.partial(on_device, mesh.shape["cent"]),
        mesh=mesh,
        in_specs=placed,
        out_specs=(P(("dp", "cent"), None), P(("dp", "cent"))),
        check_vma=False,
    )
```
